32 devices in a mesh: seq: 8 (over z, y), mp: 4 (over x, core).
Axes of the slice: x: 2, y: 2, z: 4, core: 2. Of those that a mesh axis runs over, the one named last changes fastest.
Arguments:
- hidden: bfloat16 [4, 4096, 8192], P(None, 'seq', 'mp'), may hold values from -1000 to 1000
- norm_gain: bfloat16 [4, 8192], P(None, 'mp'), may hold values from 0.25 to 1.75
- proj_weight: bfloat16 [4, 8192, 1024], P(None, 'mp'), may hold values from -0.0625 to 0.0625
- start_block: bfloat16 [8, 512, 128], replicated, may hold values from -6 to 6
Outputs:
- latents: bfloat16 [4096, 8, 128], P('seq', 'mp')
The draws below stay inside these ranges and needn't reach their ends.
All inputs are finite; a program needn't handle non-finite values.
Results may differ from the reference program's by a relative error of at most 0.025.
Values may be sent and summed in bfloat16 or wider, within the bound.
No kernel may reach another device: no remote copies, remote signals or barrier semaphores. Data moves between devices by JAX's collectives and lax.ppermute only.
A program may use at most 64 MiB of HBM per device.

```python
import jax
import jax.numpy as jnp
from jax import lax

D = 8192
HEADS = 4
HD = 128
LAYERS = 4
RANK = 128
ITERS = 2
PREFIX_TOKENS = 4096
STREAMS = 8
N_MP = 4


def draw_hidden(key, part):
    subkeys = jax.random.split(key, 4)
    position = jnp.arange(D, dtype=jnp.float32) / D
    jitter = jnp.exp(jax.random.uniform(subkeys[2], (D,), jnp.float32, -0.35, 0.35))
    common = jax.random.normal(subkeys[0], (PREFIX_TOKENS, D), jnp.float32)
    own_part = jax.random.normal(subkeys[1], (LAYERS, PREFIX_TOKENS, D), jnp.float32)
    columns = 10.0 ** position * jitter
    row_scale = 10.0 ** jax.random.uniform(subkeys[3], (LAYERS, PREFIX_TOKENS, 1), jnp.float32, 0.0, 1.0)
    base_value = 0.6 * common[None, :, :] + 0.8 * own_part
    drawn = jnp.clip(base_value * columns[None, None, :] * row_scale, -1000.0, 1000.0)
    return drawn.astype(jnp.bfloat16)


def level_of(key, dims, cuts, smallest, high):
    loudness = 1.0
    for dim, shards_of in cuts:
        heights = jax.random.uniform(jax.random.fold_in(jax.random.fold_in(key, 6), dim), (shards_of,), jnp.float32, smallest / len(cuts), high / len(cuts))
        loudness = loudness * jnp.repeat(jnp.exp(heights), dims[dim] // shards_of).reshape((-1,) + (1,) * (len(dims) - 1 - dim))
    return loudness


def normal_values(stream_key, dims, deviation, bound, shards=(), held_as=jnp.bfloat16):
    result = deviation * jax.random.normal(stream_key, dims, jnp.float32)
    if shards:
        result = result * level_of(stream_key, dims, shards, -0.22, 0.18)
    return jnp.clip(result, -bound, bound).astype(held_as)


def setup_inputs(seed: int = 0) -> dict:
    keys = jax.random.split(jax.random.key(seed), 5)
    hidden = draw_hidden(jax.random.fold_in(keys[4], 71), 0)
    norm_gain = jnp.clip(1.0 + 0.15 * jax.random.normal(keys[1], (LAYERS, D), jnp.float32), 0.25, 1.75).astype(jnp.bfloat16)
    proj_weight = normal_values(keys[2], (LAYERS, D, STREAMS * HD), D ** -0.5, 0.0625, ((1, 4),))
    start_block = normal_values(keys[3], (STREAMS, LAYERS * HD, RANK), 1.0, 6.0)
    return dict(hidden=hidden, norm_gain=norm_gain, proj_weight=proj_weight, start_block=start_block)


epsilon = 1e-05
highest_precision = lax.Precision.HIGHEST

def orthonormal_basis(image_block):
    inner_block = jnp.einsum('sar,saq->srq', image_block, image_block, precision=highest_precision)
    lower_factor = jnp.linalg.cholesky(inner_block)
    solved = jax.scipy.linalg.solve_triangular(lower_factor, jnp.swapaxes(image_block, 1, 2), lower=True)
    return jnp.swapaxes(solved, 1, 2)

def reference(hidden, norm_gain, proj_weight, start_block):
    width_here = D // N_MP
    layer_keys = []
    for layer in range(LAYERS):
        rows_full = hidden[layer].astype(jnp.float32)
        mean_square = lax.optimization_barrier(jnp.mean(rows_full * rows_full, axis=1, keepdims=True))
        normed = (rows_full * lax.rsqrt(mean_square + epsilon) * norm_gain[layer].astype(jnp.float32)[None, :]).astype(jnp.bfloat16)
        running = jnp.zeros((PREFIX_TOKENS, 2 * HEADS * HD), jnp.float32)
        for block_index in range(N_MP):
            first_col = block_index * width_here
            partial_sum = jnp.dot(normed[:, first_col:first_col + width_here].astype(jnp.float32), proj_weight[layer, first_col:first_col + width_here, :].astype(jnp.float32), preferred_element_type=jnp.float32)
            rounded = lax.optimization_barrier(partial_sum.astype(jnp.bfloat16))
            running = running + rounded.astype(jnp.float32)
        layer_keys.append(running.astype(jnp.bfloat16).reshape(PREFIX_TOKENS, 2 * HEADS, HD))
    stacked = jnp.stack(layer_keys, axis=2).reshape(PREFIX_TOKENS, 2 * HEADS, LAYERS * HD)
    widened = stacked.astype(jnp.float32)
    total_gram_matrix = jnp.einsum('tsa,tsb->sab', widened, widened, precision=highest_precision)
    block_of_basis = start_block.astype(jnp.float32)
    for repeat in range(ITERS):
        block_of_basis = orthonormal_basis(jnp.einsum('zcv,zvt->zct', total_gram_matrix, block_of_basis, precision=highest_precision))
    basis_half = block_of_basis.astype(jnp.bfloat16)
    return jnp.einsum('tsa,sar->tsr', widened, basis_half.astype(jnp.float32), precision=highest_precision).astype(jnp.bfloat16)
```

```python
import functools

import jax
import jax.numpy as jnp
from jax import lax
from jax.experimental import pallas as pl
from jax.experimental.pallas import tpu as pltpu
from jax.sharding import PartitionSpec as P

HD = 128
ITERS = 2
EPSILON = 1e-05
F32 = jnp.float32
BF16 = jnp.bfloat16
HIGHEST = lax.Precision.HIGHEST
MIB = 1 << 20


def halving_order(count):
    bits = count.bit_length() - 1
    return sorted(range(count), key=lambda r: int(format(r, f"0{bits}b")[::-1], 2)) if bits else [0]


def exchange(x, axis, bit):
    size = lax.axis_size(axis)
    return lax.ppermute(x, axis, [(j, j ^ bit) for j in range(size)])


def partial_kernel(first, steps, count, with_squares, m_ref, hid_ref, gain_ref, *refs):
    w_refs, refs = refs[:count], refs[count:]
    keep_ref, send_ref = refs[:2]
    sq_ref = refs[2] if with_squares else None
    acc_ref, sqacc_ref = refs[-2:]
    layer, k = pl.program_id(0), pl.program_id(1)
    gains = gain_ref[...].astype(F32)
    which = lax.broadcasted_iota(jnp.int32, gains.shape, 0)
    gain = jnp.sum(jnp.where(which == first + layer, gains, 0.0), axis=0, keepdims=True)
    rows = hid_ref[0].astype(F32)
    weights = jnp.concatenate([w[0] for w in w_refs], axis=1)
    product = jnp.dot((rows * gain).astype(BF16), weights, preferred_element_type=F32)

    @pl.when(k == 0)
    def _():
        acc_ref[...] = product

    @pl.when(k > 0)
    def _():
        acc_ref[...] += product

    if with_squares:
        square = rows * rows
        part = sum(square[:, i * 128 : (i + 1) * 128] for i in range(square.shape[1] // 128))

        @pl.when(k == 0)
        def _():
            sqacc_ref[...] = part

        @pl.when(k > 0)
        def _():
            sqacc_ref[...] += part

    @pl.when(k == steps - 1)
    def _():
        half = acc_ref.shape[1] // 2
        keep_ref[0] = acc_ref[:, :half].astype(BF16)
        send_ref[0] = acc_ref[:, half:].astype(BF16)
        if with_squares:
            sq_ref[0] = lax.dot_general(
                jnp.ones((8, 128), F32),
                sqacc_ref[...],
                (((1,), (1,)), ((), ())),
                precision=HIGHEST,
                preferred_element_type=F32,
            )


def partial_products(hidden, gains, weights, me, slot, layers, own, with_squares):
    _, tokens, width = hidden.shape
    mp = lax.axis_size("mp")
    order = halving_order(mp)
    block = min(width, 512)
    steps = width // block
    first, count = layers[0], len(layers)
    half = mp // 2 * HD

    def columns(r):
        return lambda layer, k, m: (first + layer, k, own * (m[0] ^ r) + slot)

    outs = [jax.ShapeDtypeStruct((count, tokens, half), BF16)] * 2
    out_specs = [pl.BlockSpec((1, tokens, half), lambda layer, k, m: (layer, 0, 0))] * 2
    if with_squares:
        outs.append(jax.ShapeDtypeStruct((count, 8, tokens), F32))
        out_specs.append(pl.BlockSpec((1, 8, tokens), lambda layer, k, m: (layer, 0, 0)))
    return pl.pallas_call(
        functools.partial(partial_kernel, first, steps, mp, with_squares),
        out_shape=outs,
        grid_spec=pltpu.PrefetchScalarGridSpec(
            num_scalar_prefetch=1,
            grid=(count, steps),
            in_specs=[
                pl.BlockSpec((1, tokens, block), lambda layer, k, m: (first + layer, 0, k)),
                pl.BlockSpec((hidden.shape[0], block), lambda layer, k, m: (0, k)),
            ]
            + [pl.BlockSpec((1, block, HD), columns(r)) for r in order],
            out_specs=out_specs,
            scratch_shapes=[
                pltpu.VMEM((tokens, mp * HD), F32),
                pltpu.VMEM((tokens, 128), F32),
            ],
        ),
        compiler_params=pltpu.CompilerParams(vmem_limit_bytes=24 * MIB),
        cost_estimate=pl.CostEstimate(
            flops=2 * count * tokens * width * mp * HD,
            bytes_accessed=count * width * (tokens + mp * HD) * 2,
            transcendentals=0,
        ),
        name=f"partial_s{slot}_l{first}",
    )(me, hidden, gains, *([weights] * mp))


def gram_kernel(shapes, width, squares_ref, *refs):
    stacked_ref, gram_ref = refs[-2:]
    refs = refs[:-2]
    layers = squares_ref.shape[0]
    factor = lax.rsqrt(squares_ref[...] / width + EPSILON)
    factor = jnp.transpose(factor.reshape(layers * 8, -1))
    at, blocks = 0, []
    for count, parts in shapes:
        for i in range(count):
            total = sum(refs[at + j][i].astype(F32) for j in range(parts))
            layer = len(blocks)
            blocks.append((total * factor[:, 8 * layer : 8 * layer + 1]).astype(BF16))
        at += parts
    stacked = jnp.concatenate(blocks, axis=1)
    stacked_ref[...] = stacked
    column = 0
    for i, block in enumerate(blocks):
        upto = (i + 1) * HD
        gram_ref[:, column : column + upto] = lax.dot_general(
            block, stacked[:, :upto], (((0,), (0,)), ((), ())), preferred_element_type=F32
        ).astype(BF16)
        column += upto


def stacked_and_gram(contributions, squares, width):
    layers, _, tokens = squares.shape
    shapes = [(parts[0].shape[0], len(parts)) for parts in contributions]
    arrays = [a for parts in contributions for a in parts]
    packed = layers * (layers + 1) // 2 * HD
    return pl.pallas_call(
        functools.partial(gram_kernel, shapes, width),
        out_shape=[
            jax.ShapeDtypeStruct((tokens, layers * HD), BF16),
            jax.ShapeDtypeStruct((HD, packed), BF16),
        ],
        grid=(1,),
        in_specs=[pl.BlockSpec(squares.shape, lambda i: (0, 0, 0))]
        + [pl.BlockSpec((a.shape[0], tokens, HD), lambda i: (0, 0, 0)) for a in arrays],
        out_specs=[
            pl.BlockSpec((tokens, layers * HD), lambda i: (0, 0)),
            pl.BlockSpec((HD, packed), lambda i: (0, 0)),
        ],
        compiler_params=pltpu.CompilerParams(vmem_limit_bytes=24 * MIB),
        name="stacked_gram",
    )(squares, *arrays)


def sum_over_seq(x):
    size = lax.axis_size("seq")
    me = lax.axis_index("seq")
    bits = [1 << i for i in range(size.bit_length() - 1)]
    for bit in bits[:-1]:
        half = x.shape[0] // 2
        mine = jnp.where((me & bit) != 0, half, 0)
        got = exchange(lax.dynamic_slice_in_dim(x, half - mine, half, 0).astype(BF16), "seq", bit)
        x = lax.dynamic_slice_in_dim(x, mine, half, 0).astype(F32) + got.astype(F32)
    x = x.astype(BF16)
    x = (x.astype(F32) + exchange(x, "seq", bits[-1]).astype(F32)).astype(BF16)
    for bit in bits[:-1][::-1]:
        got = exchange(x, "seq", bit)
        upper = (me & bit) != 0
        x = jnp.concatenate([jnp.where(upper, got, x), jnp.where(upper, x, got)], axis=0)
    return x


def split3(x):
    high = x.astype(BF16)
    rest = x - high.astype(F32)
    middle = rest.astype(BF16)
    return high, middle, (rest - middle.astype(F32)).astype(BF16)


def rank_update(x):
    h, m, l = split3(x)
    left = jnp.concatenate([h, h, m, h, m, l], axis=0)
    right = jnp.concatenate([h, m, h, l, m, h], axis=0)
    return lax.dot_general(left, right, (((0,), (0,)), ((), ())), preferred_element_type=F32)


def reciprocal(d):
    r = pl.reciprocal(d, approx=True)
    return r * (2.0 - d * r)


def factor_panel(rows, base):
    b, n = rows.shape
    lane = lax.broadcasted_iota(jnp.int32, (b, n), 1)
    row = lax.broadcasted_iota(jnp.int32, (b, n), 0)
    columns = [jnp.broadcast_to(rows[:, base + j : base + j + 1], (b, n)) for j in range(b)]
    pivots = jnp.zeros((b, n), F32)
    for k in range(b):
        pivot = jnp.broadcast_to(columns[k][k : k + 1, :], (b, n))
        pivots = jnp.where(row == k, pivot, pivots)
        here = lane == base + k
        rows = jnp.where(here & (row >= k), jnp.where(row == k, 1.0, 0.0), rows)
        if k < b - 1:
            multiplier = jnp.where(row > k, columns[k] * reciprocal(pivot), 0.0)
            rows = rows - multiplier * jnp.broadcast_to(rows[k : k + 1, :], (b, n))
            for j in range(k + 1, b):
                columns[j] = columns[j] - multiplier * jnp.broadcast_to(columns[j][k : k + 1, :], (b, n))
    rows = jnp.where((lane > base + row) & (lane < base + b), 0.0, rows)
    return rows * lax.rsqrt(pivots)


def inverse_cholesky(matrices, b=16):
    n = matrices[0].shape[0]
    panels = [[] for _ in matrices]
    rests = list(matrices)
    lane = lax.broadcasted_iota(jnp.int32, (n, n), 1)
    row = lax.broadcasted_iota(jnp.int32, (n, n), 0)
    for base in range(0, n, b):
        for s, rest in enumerate(rests):
            panels[s].append(factor_panel(rest[:b], base))
        if base + b < n:
            for s, rest in enumerate(rests):
                update = rank_update(panels[s][-1])[base + b :]
                rest = rest[b:]
                at = lane[: rest.shape[0]]
                rests[s] = jnp.where((at >= base) & (at < base + b), 0.0, rest) - update
    return [jnp.where(lane <= row, jnp.concatenate(p, axis=0), 0.0) for p in panels]


def basis_kernel(own, layers, m_ref, start_ref, *refs):
    gram_refs, stacked_refs, out_ref = refs[:own], refs[own : 2 * own], refs[2 * own]
    grams = []
    for ref in gram_refs:
        block = {}
        column = 0
        for i in range(layers):
            for j in range(i + 1):
                block[i, j] = ref[:, column : column + HD]
                column += HD
        rows = []
        for i in range(layers):
            rows.append(
                jnp.concatenate(
                    [
                        block[i, j] if j <= i else jnp.transpose(block[j, i].astype(F32)).astype(BF16)
                        for j in range(layers)
                    ],
                    axis=1,
                )
            )
        grams.append(jnp.concatenate(rows, axis=0))
    rank = start_ref.shape[2]
    images = [jnp.dot(grams[s], start_ref[s], preferred_element_type=F32) for s in range(own)]
    for step in range(ITERS):
        if step:
            images = [
                jnp.dot(grams[s], jnp.concatenate(split3(images[s]), axis=1), preferred_element_type=F32)
                for s in range(own)
            ]
            images = [x[:, :rank] + x[:, rank : 2 * rank] + x[:, 2 * rank :] for x in images]
        inner = [
            lax.dot_general(x, x, (((0,), (0,)), ((), ())), precision=HIGHEST, preferred_element_type=F32)
            for x in images
        ]
        inverse = inverse_cholesky(inner)
        images = [
            lax.dot_general(x, f, (((1,), (1,)), ((), ())), precision=HIGHEST, preferred_element_type=F32)
            for x, f in zip(images, inverse)
        ]
    for s in range(own):
        out_ref[:, s * HD : (s + 1) * HD] = jnp.dot(
            stacked_refs[s][...], images[s].astype(BF16), preferred_element_type=F32
        ).astype(BF16)


def latents_of(start, grams, stacked, me):
    own = len(grams)
    tokens = stacked[0].shape[0]
    layers = stacked[0].shape[1] // HD
    whole = lambda a: pl.BlockSpec(a.shape, lambda i, m: (0, 0))
    return pl.pallas_call(
        functools.partial(basis_kernel, own, layers),
        out_shape=jax.ShapeDtypeStruct((tokens, own * HD), BF16),
        grid_spec=pltpu.PrefetchScalarGridSpec(
            num_scalar_prefetch=1,
            grid=(1,),
            in_specs=[pl.BlockSpec((own,) + start.shape[1:], lambda i, m: (m[0], 0, 0))]
            + [whole(a) for a in grams + stacked],
            out_specs=pl.BlockSpec((tokens, own * HD), lambda i, m: (0, 0)),
        ),
        compiler_params=pltpu.CompilerParams(vmem_limit_bytes=40 * MIB),
        name="basis_latents",
    )(me, start, *grams, *stacked).reshape(tokens, own, HD)


def groups_of(slot, layers, own):
    if slot + 1 < own:
        return [[0], [1], list(range(2, layers))]
    return [list(range(0, layers - 1)), [layers - 1]]


def on_device(hidden, norm_gain, proj_weight, start_block):
    layers, tokens, width = hidden.shape
    mp = lax.axis_size("mp")
    own = proj_weight.shape[2] // HD // mp
    me = lax.axis_index("mp").astype(jnp.int32).reshape(1)
    mp_bits = [1 << i for i in range(mp.bit_length() - 1)]

    squares, pieces = [], [[] for _ in range(own)]
    for slot in range(own):
        for group in groups_of(slot, layers, own):
            outs = partial_products(hidden, norm_gain, proj_weight, me, slot, group, own, slot == 0)
            if slot == 0:
                squares.append(outs[2])
            contributions = [outs[0]]
            for bit in mp_bits:
                if bit == 1:
                    send = outs[1]
                else:
                    half = contributions[-1].shape[2] // 2
                    send = sum(c[:, :, half : 2 * half].astype(F32) for c in contributions).astype(BF16)
                contributions.append(exchange(send, "mp", bit))
            pieces[slot].append(contributions)
        if slot == 0:
            totals = jnp.concatenate(squares, axis=0)
            for bit in mp_bits:
                totals = totals + exchange(totals, "mp", bit)

    grams, stacked = [], []
    for slot in range(own):
        rows, gram = stacked_and_gram(pieces[slot], totals, width * mp)
        stacked.append(rows)
        grams.append(sum_over_seq(gram))
    return latents_of(start_block, grams, stacked, me)


def solution(mesh):
    return jax.shard_map(
        on_device,
        mesh=mesh,
        in_specs=(P(None, "seq", "mp"), P(None, "mp"), P(None, "mp", None), P()),
        out_specs=P("seq", "mp", None),
        check_vma=False,
    )
```

```python
import functools

import jax
import jax.numpy as jnp
from jax import lax
from jax.experimental import pallas as pl
from jax.experimental.pallas import tpu as pltpu
from jax.sharding import PartitionSpec as P

HD = 128
ITERS = 2
EPSILON = 1e-05
F32 = jnp.float32
BF16 = jnp.bfloat16
HIGHEST = lax.Precision.HIGHEST
MIB = 1 << 20


def halving_order(count):
    bits = count.bit_length() - 1
    return sorted(range(count), key=lambda r: int(format(r, f"0{bits}b")[::-1], 2)) if bits else [0]


def exchange(x, axis, bit):
    size = lax.axis_size(axis)
    return lax.ppermute(x, axis, [(j, j ^ bit) for j in range(size)])


def partial_kernel(own, parcels, m_ref, gain_ref, hid_ref, w_ref, *refs):
    outs, squares_ref = refs[: 2 * len(parcels)], refs[2 * len(parcels)]
    rows_ref, cols_ref, sems = refs[-3:]
    layers, tokens, width = rows_ref.shape
    mp = cols_ref.shape[2] // HD // own
    order = halving_order(mp)
    place = {}
    for i, (slot, members) in enumerate(parcels):
        for j, layer in enumerate(members):
            place[slot, layer] = (outs[2 * i].at[j], outs[2 * i + 1].at[j])
    copies = {}
    for layer in range(layers):
        here = [pltpu.make_async_copy(hid_ref.at[layer], rows_ref.at[layer], sems.at[layer, 0])]
        for slot in range(own):
            for i, r in enumerate(order):
                column = pl.multiple_of((own * (m_ref[0] ^ r) + slot) * HD, HD)
                to = slot * mp + i
                here.append(
                    pltpu.make_async_copy(
                        w_ref.at[layer, :, pl.ds(column, HD)],
                        cols_ref.at[layer, :, pl.ds(to * HD, HD)],
                        sems.at[layer, 1 + to],
                    )
                )
        for copy in here:
            copy.start()
        copies[layer] = here
    half = mp // 2 * HD
    gains = gain_ref[...]
    for layer in range(layers):
        copies[layer][0].wait()
        rows = rows_ref[layer]
        scaled = rows * gains[layer : layer + 1]
        totals = []
        for slot in range(own):
            for copy in copies[layer][1 + slot * mp : 1 + (slot + 1) * mp]:
                copy.wait()
            weights = cols_ref[layer, :, slot * mp * HD : (slot + 1) * mp * HD]
            totals.append(jnp.dot(scaled, weights, preferred_element_type=F32))
        wide = rows.astype(F32)
        squares = None
        for i in range(width // HD):
            x = wide[:, i * HD : (i + 1) * HD]
            squares = x * x if squares is None else squares + x * x
        for slot in range(own):
            keep, send = place[slot, layer]
            keep[...] = totals[slot][:, :half].astype(BF16)
            send[...] = totals[slot][:, half:].astype(BF16)
        squares_ref[layer : layer + 1, :] = lax.dot_general(
            jnp.ones((8, HD), F32),
            squares,
            (((1,), (1,)), ((), ())),
            precision=HIGHEST,
            preferred_element_type=F32,
        )[:1]


def partial_products(hidden, gains, weights, me, own, parcels):
    layers, tokens, width = hidden.shape
    mp = lax.axis_size("mp")
    half = mp // 2 * HD
    outs = [jax.ShapeDtypeStruct((len(members), tokens, half), BF16) for _, members in parcels for _ in range(2)]
    outs.append(jax.ShapeDtypeStruct((layers, tokens), F32))
    vmem = pl.BlockSpec(memory_space=pltpu.VMEM)
    hbm = pl.BlockSpec(memory_space=pltpu.HBM)
    return pl.pallas_call(
        functools.partial(partial_kernel, own, parcels),
        out_shape=outs,
        in_specs=[pl.BlockSpec(memory_space=pltpu.SMEM), vmem, hbm, hbm],
        out_specs=[vmem] * len(outs),
        scratch_shapes=[
            pltpu.VMEM((layers, tokens, width), BF16),
            pltpu.VMEM((layers, width, own * mp * HD), BF16),
            pltpu.SemaphoreType.DMA((layers, own * mp + 1)),
        ],
        compiler_params=pltpu.CompilerParams(vmem_limit_bytes=32 * MIB),
        cost_estimate=pl.CostEstimate(
            flops=2 * layers * tokens * width * own * mp * HD,
            bytes_accessed=layers * width * (tokens + own * mp * HD) * 2,
            transcendentals=0,
        ),
        name="partial_products",
    )(me, gains, *[pltpu.with_memory_space_constraint(x, pltpu.HBM) for x in (hidden, weights)])


def extra_rows(tokens):
    return -(-3 * (tokens // HD) // 16) * 16


def merge_kernel(parts, tokens, with_totals, *refs):
    own_ref, out_ref = refs[-2:]
    layers, _, half = out_ref.shape
    for layer in range(layers):
        total = sum(r[layer].astype(F32) for r in refs[:parts])
        own_ref[layer] = total[:, :half].astype(BF16)
        out_ref[layer, :tokens, :] = total[:, half:].astype(BF16)
    if with_totals:
        totals = refs[parts][...]
        cuts = tokens // HD
        rows = out_ref.shape[1] - tokens
        for layer in range(layers):
            line = jnp.concatenate([totals[layer : layer + 1, i * HD : (i + 1) * HD] for i in range(cuts)], axis=0)
            pieces = [p.astype(F32) for p in split3(line)]
            pad = [jnp.zeros((rows - 3 * cuts, HD), F32)] if rows > 3 * cuts else []
            block = jnp.concatenate(pieces + pad, axis=0).astype(BF16)
            out_ref[layer, tokens:, :HD] = block
            if out_ref.shape[2] > HD:
                out_ref[layer, tokens:, HD:] = jnp.zeros((rows, out_ref.shape[2] - HD), BF16)


def next_send(arrays, totals, tokens):
    layers, _, width = arrays[0].shape
    half = width // 2
    rows = tokens + (extra_rows(tokens) if totals is not None else 0)
    extra = [] if totals is None else [totals]
    return pl.pallas_call(
        functools.partial(merge_kernel, len(arrays), tokens, totals is not None),
        out_shape=[
            jax.ShapeDtypeStruct((layers, tokens, half), BF16),
            jax.ShapeDtypeStruct((layers, rows, half), BF16),
        ],
        grid=(1,),
        in_specs=[pl.BlockSpec((layers, tokens, width), lambda i: (0, 0, 0)) for _ in arrays]
        + [pl.BlockSpec(t.shape, lambda i: (0, 0)) for t in extra],
        out_specs=[
            pl.BlockSpec((layers, tokens, half), lambda i: (0, 0, 0)),
            pl.BlockSpec((layers, rows, half), lambda i: (0, 0, 0)),
        ],
        compiler_params=pltpu.CompilerParams(vmem_limit_bytes=16 * MIB),
        name="next_send",
    )(*arrays, *extra)


def carried_totals(received, tokens):
    cuts = tokens // HD
    pieces = received[:, tokens : tokens + 3 * cuts, :HD].astype(F32)
    return pieces.reshape(-1, 3, tokens).sum(1)


def gram_kernel(shapes, width, squares_ref, *refs):
    stacked_ref, gram_ref = refs[-2:]
    refs = refs[:-2]
    layers = squares_ref.shape[0]
    factor = lax.rsqrt(squares_ref[...] / width + EPSILON)
    factor = jnp.transpose(jnp.concatenate([factor] * (8 // layers), axis=0))
    at, blocks = 0, []
    for count, parts in shapes:
        for i in range(count):
            total = sum(refs[at + j][i].astype(F32) for j in range(parts))
            layer = len(blocks)
            blocks.append((total * factor[:, layer : layer + 1]).astype(BF16))
        at += parts
    stacked = jnp.concatenate(blocks, axis=1)
    stacked_ref[...] = stacked
    column = 0
    for i, block in enumerate(blocks):
        upto = (i + 1) * HD
        gram_ref[:, column : column + upto] = lax.dot_general(
            block, stacked[:, :upto], (((0,), (0,)), ((), ())), preferred_element_type=F32
        ).astype(BF16)
        column += upto


def stacked_and_gram(contributions, squares, width):
    layers, tokens = squares.shape
    shapes = [(parts[0].shape[0], len(parts)) for parts in contributions]
    arrays = [a for parts in contributions for a in parts]
    packed = layers * (layers + 1) // 2 * HD
    return pl.pallas_call(
        functools.partial(gram_kernel, shapes, width),
        out_shape=[
            pltpu.HBM((tokens, layers * HD), BF16),
            jax.ShapeDtypeStruct((HD, packed), BF16),
        ],
        grid=(1,),
        in_specs=[pl.BlockSpec(squares.shape, lambda i: (0, 0))]
        + [pl.BlockSpec((a.shape[0], tokens, HD), lambda i: (0, 0, 0)) for a in arrays],
        out_specs=[
            pl.BlockSpec((tokens, layers * HD), lambda i: (0, 0)),
            pl.BlockSpec((HD, packed), lambda i: (0, 0)),
        ],
        compiler_params=pltpu.CompilerParams(vmem_limit_bytes=16 * MIB),
        name="stacked_gram",
    )(squares, *arrays)


def sum_over_seq(x):
    size = lax.axis_size("seq")
    me = lax.axis_index("seq")
    bits = [1 << i for i in range(size.bit_length() - 1)]
    for bit in bits[:-1]:
        half = x.shape[0] // 2
        mine = jnp.where((me & bit) != 0, half, 0)
        got = exchange(lax.dynamic_slice_in_dim(x, half - mine, half, 0).astype(BF16), "seq", bit)
        x = lax.dynamic_slice_in_dim(x, mine, half, 0).astype(F32) + got.astype(F32)
    x = x.astype(BF16)
    x = (x.astype(F32) + exchange(x, "seq", bits[-1]).astype(F32)).astype(BF16)
    for bit in bits[:-1][::-1]:
        got = exchange(x, "seq", bit)
        upper = (me & bit) != 0
        x = jnp.concatenate([jnp.where(upper, got, x), jnp.where(upper, x, got)], axis=0)
    return x


def split3(x):
    high = x.astype(BF16)
    rest = x - high.astype(F32)
    middle = rest.astype(BF16)
    return high, middle, (rest - middle.astype(F32)).astype(BF16)


def rank_update(x):
    h, m, l = split3(x)
    left = jnp.concatenate([h, h, m, h, m, l], axis=0)
    right = jnp.concatenate([h, m, h, l, m, h], axis=0)
    return lax.dot_general(left, right, (((0,), (0,)), ((), ())), preferred_element_type=F32)


def reciprocal(d):
    r = pl.reciprocal(d, approx=True)
    return r * (2.0 - d * r)


def factor_panel(rows, base):
    b, n = rows.shape
    lane = lax.broadcasted_iota(jnp.int32, (b, n), 1)
    row = lax.broadcasted_iota(jnp.int32, (b, n), 0)
    columns = [jnp.broadcast_to(rows[:, base + j : base + j + 1], (b, n)) for j in range(b)]
    pivots = jnp.zeros((b, n), F32)
    for k in range(b):
        pivot = jnp.broadcast_to(columns[k][k : k + 1, :], (b, n))
        pivots = jnp.where(row == k, pivot, pivots)
        here = lane == base + k
        rows = jnp.where(here & (row >= k), jnp.where(row == k, 1.0, 0.0), rows)
        if k < b - 1:
            multiplier = jnp.where(row > k, columns[k] * reciprocal(pivot), 0.0)
            rows = rows - multiplier * jnp.broadcast_to(rows[k : k + 1, :], (b, n))
            for j in range(k + 1, b):
                columns[j] = columns[j] - multiplier * jnp.broadcast_to(columns[j][k : k + 1, :], (b, n))
    rows = jnp.where((lane > base + row) & (lane < base + b), 0.0, rows)
    return rows * lax.rsqrt(pivots)


def inverse_cholesky(matrices, b=16):
    n = matrices[0].shape[0]
    panels = [[] for _ in matrices]
    rests = list(matrices)
    lane = lax.broadcasted_iota(jnp.int32, (n, n), 1)
    row = lax.broadcasted_iota(jnp.int32, (n, n), 0)
    for base in range(0, n, b):
        for s, rest in enumerate(rests):
            panels[s].append(factor_panel(rest[:b], base))
        if base + b < n:
            for s, rest in enumerate(rests):
                update = rank_update(panels[s][-1])[base + b :]
                rest = rest[b:]
                at = lane[: rest.shape[0]]
                rests[s] = jnp.where((at >= base) & (at < base + b), 0.0, rest) - update
    return [jnp.where(lane <= row, jnp.concatenate(p, axis=0), 0.0) for p in panels]


def basis_kernel(own, layers, start_ref, *refs):
    gram_refs, stacked_refs, out_ref = refs[:own], refs[own : 2 * own], refs[2 * own]
    rows_ref, sems = refs[2 * own + 1 :]
    copies = [pltpu.make_async_copy(stacked_refs[s], rows_ref.at[s], sems.at[s]) for s in range(own)]
    for copy in copies:
        copy.start()
    grams = []
    for ref in gram_refs:
        block = {}
        column = 0
        for i in range(layers):
            for j in range(i + 1):
                block[i, j] = ref[:, column : column + HD]
                column += HD
        rows = []
        for i in range(layers):
            rows.append(
                jnp.concatenate(
                    [
                        block[i, j] if j <= i else jnp.transpose(block[j, i].astype(F32)).astype(BF16)
                        for j in range(layers)
                    ],
                    axis=1,
                )
            )
        grams.append(jnp.concatenate(rows, axis=0))
    rank = start_ref.shape[2]
    images = [jnp.dot(grams[s], start_ref[s], preferred_element_type=F32) for s in range(own)]
    for step in range(ITERS):
        if step:
            images = [
                jnp.dot(grams[s], jnp.concatenate(split3(images[s]), axis=1), preferred_element_type=F32)
                for s in range(own)
            ]
            images = [x[:, :rank] + x[:, rank : 2 * rank] + x[:, 2 * rank :] for x in images]
        inner = [
            lax.dot_general(x, x, (((0,), (0,)), ((), ())), precision=HIGHEST, preferred_element_type=F32)
            for x in images
        ]
        inverse = inverse_cholesky(inner)
        images = [
            lax.dot_general(x, f, (((1,), (1,)), ((), ())), precision=HIGHEST, preferred_element_type=F32)
            for x, f in zip(images, inverse)
        ]
    for s in range(own):
        copies[s].wait()
        out_ref[:, s, :] = jnp.dot(
            rows_ref[s], images[s].astype(BF16), preferred_element_type=F32
        ).astype(BF16)


def latents_of(start, grams, stacked):
    own = len(grams)
    tokens = stacked[0].shape[0]
    layers = stacked[0].shape[1] // HD
    whole = lambda a: pl.BlockSpec(a.shape, lambda i: (0,) * a.ndim)
    return pl.pallas_call(
        functools.partial(basis_kernel, own, layers),
        out_shape=jax.ShapeDtypeStruct((tokens, own, HD), BF16),
        grid=(1,),
        in_specs=[whole(a) for a in [start] + grams] + [pl.BlockSpec(memory_space=pltpu.HBM)] * own,
        out_specs=pl.BlockSpec((tokens, own, HD), lambda i: (0, 0, 0)),
        scratch_shapes=[pltpu.VMEM((own,) + stacked[0].shape, BF16), pltpu.SemaphoreType.DMA((own,))],
        compiler_params=pltpu.CompilerParams(vmem_limit_bytes=16 * MIB),
        name="basis_latents",
    )(start, *grams, *[pltpu.with_memory_space_constraint(x, pltpu.HBM) for x in stacked])


def parcels_of(layers, own):
    return [(slot, list(range(layers))) for slot in range(own)]


def on_device(hidden, norm_gain, proj_weight, start_block):
    layers, tokens, width = hidden.shape
    mp = lax.axis_size("mp")
    own = proj_weight.shape[2] // HD // mp
    me = lax.axis_index("mp").astype(jnp.int32).reshape(1)
    mp_bits = [1 << i for i in range(mp.bit_length() - 1)]

    outs = partial_products(hidden, norm_gain, proj_weight, me, own, parcels_of(layers, own))
    totals = outs[-1]
    pieces = [[outs[2 * slot]] for slot in range(own)]
    for bit in mp_bits:
        for slot in range(own):
            if bit == 1:
                got = exchange(outs[2 * slot + 1], "mp", bit)
                if slot == 0:
                    totals = totals + exchange(totals, "mp", bit)
            else:
                own_sum, send = next_send(pieces[slot], totals if slot == 0 else None, tokens)
                pieces[slot] = [own_sum]
                got = exchange(send, "mp", bit)
                if slot == 0:
                    totals = totals + carried_totals(got, tokens)
            pieces[slot].append(got)
    pieces = [[parts] for parts in pieces]

    grams, stacked = [], []
    for slot in range(own):
        rows, gram = stacked_and_gram(pieces[slot], totals, width * mp)
        stacked.append(rows)
        grams.append(sum_over_seq(gram))
    start = lax.dynamic_slice_in_dim(start_block, me[0] * own, own, 0)
    return latents_of(start, grams, stacked)


def solution(mesh):
    return jax.shard_map(
        on_device,
        mesh=mesh,
        in_specs=(P(None, "seq", "mp"), P(None, "mp"), P(None, "mp", None), P()),
        out_specs=P("seq", "mp", None),
        check_vma=False,
    )
```

```python
import functools

import jax
import jax.numpy as jnp
from jax import lax
from jax.experimental import pallas as pl
from jax.experimental.pallas import tpu as pltpu
from jax.sharding import PartitionSpec as P

HD = 128
ITERS = 2
EPSILON = 1e-05
F32 = jnp.float32
BF16 = jnp.bfloat16
HIGHEST = lax.Precision.HIGHEST
MIB = 1 << 20
LEAD = 0


def halving_order(count):
    bits = count.bit_length() - 1
    return sorted(range(count), key=lambda r: int(format(r, f"0{bits}b")[::-1], 2)) if bits else [0]


def exchange(x, axis, bit):
    size = lax.axis_size(axis)
    return lax.ppermute(x, axis, [(j, j ^ bit) for j in range(size)])


def partial_kernel(own, slot, cuts, with_squares, m_ref, gain_ref, hid_ref, w_ref, *refs):
    rows_ref, cols_ref, sems = refs[-3:]
    layers, tokens, width = rows_ref.shape
    mp = cols_ref.shape[2] // HD
    order = halving_order(mp)
    send = [(ref, i) for ref, count in zip(refs[1:], cuts) for i in range(count)]
    copies = {}
    for layer in range(layers):
        here = [pltpu.make_async_copy(hid_ref.at[layer], rows_ref.at[layer], sems.at[layer, 0])]
        for i, r in enumerate(order):
            column = pl.multiple_of((own * (m_ref[0] ^ r) + slot) * HD, HD)
            here.append(
                pltpu.make_async_copy(
                    w_ref.at[layer, :, pl.ds(column, HD)],
                    cols_ref.at[layer, :, pl.ds(i * HD, HD)],
                    sems.at[layer, 1 + i],
                )
            )
        for copy in here:
            copy.start()
        copies[layer] = here
    half = mp // 2 * HD
    gains = gain_ref[...]
    for layer in range(layers):
        copies[layer][0].wait()
        rows = rows_ref[layer]
        scaled = rows * gains[layer : layer + 1]
        for copy in copies[layer][1:]:
            copy.wait()
        total = jnp.dot(scaled, cols_ref[layer], preferred_element_type=F32)
        refs[0][layer] = total[:, :half].astype(BF16)
        ref, i = send[layer]
        ref[i] = total[:, half:].astype(BF16)
        if not with_squares:
            continue
        wide = rows.astype(F32)
        squares = None
        for i in range(width // HD):
            x = wide[:, i * HD : (i + 1) * HD]
            squares = x * x if squares is None else squares + x * x
        refs[1 + len(cuts)][layer : layer + 1, :] = lax.dot_general(
            jnp.ones((8, HD), F32),
            squares,
            (((1,), (1,)), ((), ())),
            precision=HIGHEST,
            preferred_element_type=F32,
        )[:1]


def partial_products(hidden, gains, weights, me, own, slot, cuts, with_squares):
    layers, tokens, width = hidden.shape
    mp = lax.axis_size("mp")
    half = mp // 2 * HD
    outs = [jax.ShapeDtypeStruct((n, tokens, half), BF16) for n in [layers] + cuts]
    outs += [jax.ShapeDtypeStruct((layers, tokens), F32)] * with_squares
    vmem = pl.BlockSpec(memory_space=pltpu.VMEM)
    hbm = pl.BlockSpec(memory_space=pltpu.HBM)
    return pl.pallas_call(
        functools.partial(partial_kernel, own, slot, cuts, with_squares),
        out_shape=outs,
        in_specs=[pl.BlockSpec(memory_space=pltpu.SMEM), vmem, hbm, hbm],
        out_specs=[vmem] * len(outs),
        scratch_shapes=[
            pltpu.VMEM((layers, tokens, width), BF16),
            pltpu.VMEM((layers, width, mp * HD), BF16),
            pltpu.SemaphoreType.DMA((layers, mp + 1)),
        ],
        compiler_params=pltpu.CompilerParams(vmem_limit_bytes=32 * MIB),
        cost_estimate=pl.CostEstimate(
            flops=2 * layers * tokens * width * mp * HD,
            bytes_accessed=layers * width * (tokens + mp * HD) * 2,
            transcendentals=0,
        ),
        name="partial_products",
    )(me, gains, *[pltpu.with_memory_space_constraint(x, pltpu.HBM) for x in (hidden, weights)])


def extra_rows(tokens):
    return -(-3 * (tokens // HD) // 16) * 16


def by_layer(groups, refs):
    parts, at = [], 0
    for counts in groups:
        parts.append([refs[at + n].at[i] for n, count in enumerate(counts) for i in range(count)])
        at += len(counts)
    return parts, at


def merge_kernel(groups, tokens, cuts, with_totals, *refs):
    own_ref, out_refs = refs[-1 - len(cuts)], refs[-len(cuts) :]
    layers, _, half = own_ref.shape
    out = [(ref, i) for ref, count in zip(out_refs, cuts) for i in range(count)]
    parts, at = by_layer(groups, refs)
    for layer in range(layers):
        total = sum(p[layer][...].astype(F32) for p in parts)
        own_ref[layer] = total[:, :half].astype(BF16)
        ref, i = out[layer]
        ref[i, :tokens, :] = total[:, half:].astype(BF16)
    if with_totals:
        totals = refs[at][...]
        pieces_of = tokens // HD
        rows = out_refs[0].shape[1] - tokens
        for layer in range(layers):
            line = jnp.concatenate(
                [totals[layer : layer + 1, i * HD : (i + 1) * HD] for i in range(pieces_of)], axis=0
            )
            pieces = [p.astype(F32) for p in split3(line)]
            pad = [jnp.zeros((rows - 3 * pieces_of, HD), F32)] if rows > 3 * pieces_of else []
            ref, i = out[layer]
            ref[i, tokens:, :HD] = jnp.concatenate(pieces + pad, axis=0).astype(BF16)
            if half > HD:
                ref[i, tokens:, HD:] = jnp.zeros((rows, half - HD), BF16)


def next_send(pieces, totals, tokens, cuts):
    groups = [[a.shape[0] for a in group] for group in pieces]
    arrays = [a for group in pieces for a in group]
    layers, width = sum(groups[0]), arrays[0].shape[2]
    half = width // 2
    rows = tokens + (extra_rows(tokens) if totals is not None else 0)
    extra = [] if totals is None else [totals]
    block = lambda *shape: pl.BlockSpec(shape, lambda i: (0,) * len(shape))
    return pl.pallas_call(
        functools.partial(merge_kernel, groups, tokens, cuts, totals is not None),
        out_shape=[jax.ShapeDtypeStruct((layers, tokens, half), BF16)]
        + [jax.ShapeDtypeStruct((count, rows, half), BF16) for count in cuts],
        grid=(1,),
        in_specs=[block(a.shape[0], tokens, width) for a in arrays] + [block(*t.shape) for t in extra],
        out_specs=[block(layers, tokens, half)] + [block(count, rows, half) for count in cuts],
        compiler_params=pltpu.CompilerParams(vmem_limit_bytes=16 * MIB),
        name="next_send",
    )(*arrays, *extra)


def carried_totals(received, tokens):
    cuts = tokens // HD
    pieces = received[:, tokens : tokens + 3 * cuts, :HD].astype(F32)
    return pieces.reshape(-1, 3, tokens).sum(1)


def gram_kernel(groups, width, squares_ref, *refs):
    stacked_ref, gram_ref = refs[-2:]
    layers = squares_ref.shape[0]
    factor = lax.rsqrt(squares_ref[...] / width + EPSILON)
    factor = jnp.transpose(jnp.concatenate([factor] * (8 // layers), axis=0))
    parts, _ = by_layer(groups, refs)
    blocks = []
    for layer in range(layers):
        total = sum(p[layer][...].astype(F32) for p in parts)
        blocks.append((total * factor[:, layer : layer + 1]).astype(BF16))
    stacked = jnp.concatenate(blocks, axis=1)
    stacked_ref[...] = stacked
    column = 0
    for i, block in enumerate(blocks):
        upto = (i + 1) * HD
        gram_ref[:, column : column + upto] = lax.dot_general(
            block, stacked[:, :upto], (((0,), (0,)), ((), ())), preferred_element_type=F32
        ).astype(BF16)
        column += upto


def stacked_and_gram(pieces, squares, width):
    layers, tokens = squares.shape
    groups = [[a.shape[0] for a in group] for group in pieces]
    arrays = [a for group in pieces for a in group]
    packed = layers * (layers + 1) // 2 * HD
    return pl.pallas_call(
        functools.partial(gram_kernel, groups, width),
        out_shape=[
            pltpu.HBM((tokens, layers * HD), BF16),
            jax.ShapeDtypeStruct((HD, packed), BF16),
        ],
        grid=(1,),
        in_specs=[pl.BlockSpec(squares.shape, lambda i: (0, 0))]
        + [pl.BlockSpec((a.shape[0], tokens, HD), lambda i: (0, 0, 0)) for a in arrays],
        out_specs=[
            pl.BlockSpec((tokens, layers * HD), lambda i: (0, 0)),
            pl.BlockSpec((HD, packed), lambda i: (0, 0)),
        ],
        compiler_params=pltpu.CompilerParams(vmem_limit_bytes=16 * MIB),
        name="stacked_gram",
    )(squares, *arrays)


def sum_over_seq(x, ahead):
    size = lax.axis_size("seq")
    me = lax.axis_index("seq")
    bits = [1 << i for i in range(size.bit_length() - 1)]
    arrived = []

    def step(send, bit):
        if len(arrived) + LEAD < len(ahead) - 1:
            send = lax.optimization_barrier((send, ahead[len(arrived) + LEAD]))[0]
        arrived.append(exchange(send, "seq", bit))
        return arrived[-1]

    for bit in bits[:-1]:
        half = x.shape[0] // 2
        mine = jnp.where((me & bit) != 0, half, 0)
        got = step(lax.dynamic_slice_in_dim(x, half - mine, half, 0).astype(BF16), bit)
        x = lax.dynamic_slice_in_dim(x, mine, half, 0).astype(F32) + got.astype(F32)
    x = x.astype(BF16)
    x = (x.astype(F32) + step(x, bits[-1]).astype(F32)).astype(BF16)
    for bit in bits[:-1][::-1]:
        got = step(x, bit)
        upper = (me & bit) != 0
        x = jnp.concatenate([jnp.where(upper, got, x), jnp.where(upper, x, got)], axis=0)
    return x, arrived


def split3(x):
    high = x.astype(BF16)
    rest = x - high.astype(F32)
    middle = rest.astype(BF16)
    return high, middle, (rest - middle.astype(F32)).astype(BF16)


def rank_update(x):
    h, m, l = split3(x)
    left = jnp.concatenate([h, h, m, h, m, l], axis=0)
    right = jnp.concatenate([h, m, h, l, m, h], axis=0)
    return lax.dot_general(left, right, (((0,), (0,)), ((), ())), preferred_element_type=F32)


def reciprocal(d):
    r = pl.reciprocal(d, approx=True)
    return r * (2.0 - d * r)


def factor_panel(rows, base):
    b, n = rows.shape
    lane = lax.broadcasted_iota(jnp.int32, (8, n), 1)
    row = lax.broadcasted_iota(jnp.int32, (8, n), 0)

    def spread(x, k):
        return jnp.broadcast_to(x[k : k + 1, :], (8, n))

    tiles = [rows[i : i + 8] for i in range(0, b, 8)]
    columns = [[jnp.broadcast_to(t[:, base + j : base + j + 1], (8, n)) for t in tiles] for j in range(b)]
    pivots = [jnp.zeros((8, n), F32) for _ in tiles]
    for k in range(b):
        top, at = k // 8, k % 8
        pivot = spread(columns[k][top], at)
        pivots[top] = jnp.where(row == at, pivot, pivots[top])
        here = lane == base + k
        tiles[top] = jnp.where(here & (row >= at), jnp.where(row == at, 1.0, 0.0), tiles[top])
        if k == b - 1:
            break
        inverse = reciprocal(pivot)
        chosen = spread(tiles[top], at)
        others = [spread(columns[j][top], at) for j in range(k + 1, b)]
        for i in range(top, len(tiles)):
            multiplier = columns[k][i] * inverse
            if i == top:
                multiplier = jnp.where(row > at, multiplier, 0.0)
            else:
                tiles[i] = jnp.where(here, 0.0, tiles[i])
            tiles[i] = tiles[i] - multiplier * chosen
            for j in range(k + 1, b):
                columns[j][i] = columns[j][i] - multiplier * others[j - k - 1]
    for i in range(len(tiles)):
        tiles[i] = jnp.where((lane > base + 8 * i + row) & (lane < base + b), 0.0, tiles[i])
        tiles[i] = tiles[i] * lax.rsqrt(pivots[i])
    return jnp.concatenate(tiles, axis=0)


def inverse_cholesky(matrices, b=16):
    n = matrices[0].shape[0]
    panels = [[] for _ in matrices]
    rests = list(matrices)
    lane = lax.broadcasted_iota(jnp.int32, (n, n), 1)
    row = lax.broadcasted_iota(jnp.int32, (n, n), 0)
    for base in range(0, n, b):
        for s, rest in enumerate(rests):
            panels[s].append(factor_panel(rest[:b], base))
        if base + b < n:
            for s, rest in enumerate(rests):
                update = rank_update(panels[s][-1])[base + b :]
                rest = rest[b:]
                at = lane[: rest.shape[0]]
                rests[s] = jnp.where((at >= base) & (at < base + b), 0.0, rest) - update
    return [jnp.where(lane <= row, jnp.concatenate(p, axis=0), 0.0) for p in panels]


def basis_kernel(own, layers, start_ref, *refs):
    gram_refs, stacked_refs, out_ref = refs[:own], refs[own : 2 * own], refs[2 * own]
    rows_ref, sems = refs[2 * own + 1 :]
    copies = [pltpu.make_async_copy(stacked_refs[s], rows_ref.at[s], sems.at[s]) for s in range(own)]
    for copy in copies:
        copy.start()
    grams = []
    for ref in gram_refs:
        block = {}
        column = 0
        for i in range(layers):
            for j in range(i + 1):
                block[i, j] = ref[:, column : column + HD]
                column += HD
        rows = []
        for i in range(layers):
            rows.append(
                jnp.concatenate(
                    [
                        block[i, j] if j <= i else jnp.transpose(block[j, i].astype(F32)).astype(BF16)
                        for j in range(layers)
                    ],
                    axis=1,
                )
            )
        grams.append(jnp.concatenate(rows, axis=0))
    rank = start_ref.shape[1]

    def through_gram(x, gram):
        y = jnp.dot(jnp.concatenate(split3(x), axis=0), gram, preferred_element_type=F32)
        return y[:rank] + y[rank : 2 * rank] + y[2 * rank :]

    images = [jnp.dot(start_ref[s], grams[s], preferred_element_type=F32) for s in range(own)]
    for step in range(ITERS):
        inner = [
            lax.dot_general(x, x, (((1,), (1,)), ((), ())), precision=HIGHEST, preferred_element_type=F32)
            for x in images
        ]
        if step < ITERS - 1:
            images = [through_gram(x, g) for x, g in zip(images, grams)]
        images = [
            jnp.dot(f, x, precision=HIGHEST, preferred_element_type=F32)
            for x, f in zip(images, inverse_cholesky(inner))
        ]
    for s in range(own):
        copies[s].wait()
        out_ref[:, s, :] = lax.dot_general(
            rows_ref[s], images[s].astype(BF16), (((1,), (1,)), ((), ())), preferred_element_type=F32
        ).astype(BF16)


def latents_of(start, grams, stacked):
    own = len(grams)
    tokens = stacked[0].shape[0]
    layers = stacked[0].shape[1] // HD
    whole = lambda a: pl.BlockSpec(a.shape, lambda i: (0,) * a.ndim)
    return pl.pallas_call(
        functools.partial(basis_kernel, own, layers),
        out_shape=jax.ShapeDtypeStruct((tokens, own, HD), BF16),
        grid=(1,),
        in_specs=[whole(a) for a in [start] + grams] + [pl.BlockSpec(memory_space=pltpu.HBM)] * own,
        out_specs=pl.BlockSpec((tokens, own, HD), lambda i: (0, 0, 0)),
        scratch_shapes=[pltpu.VMEM((own,) + stacked[0].shape, BF16), pltpu.SemaphoreType.DMA((own,))],
        compiler_params=pltpu.CompilerParams(vmem_limit_bytes=16 * MIB),
        name="basis_latents",
    )(start, *grams, *[pltpu.with_memory_space_constraint(x, pltpu.HBM) for x in stacked])


def on_device(hidden, norm_gain, proj_weight, start_block):
    layers, tokens, width = hidden.shape
    mp = lax.axis_size("mp")
    own = proj_weight.shape[2] // HD // mp
    me = lax.axis_index("mp").astype(jnp.int32).reshape(1)
    mp_bits = [1 << i for i in range(mp.bit_length() - 1)]

    pieces, totals, sent = [], None, []
    for slot in range(own):
        here = me if slot == 0 else lax.optimization_barrier((me, sent[-1]))[0]
        cuts = [layers] if slot == 0 else [layers // 2, layers - layers // 2]
        held, *sent = partial_products(hidden, norm_gain, proj_weight, here, own, slot, cuts, slot == 0)
        if slot == 0:
            totals = sent.pop()
            totals = totals + exchange(totals, "mp", 1)
        got = [exchange(send, "mp", 1) for send in sent]
        for bit in mp_bits[1:]:
            cuts = [layers] if slot == 0 or bit != mp_bits[-1] else [layers // 2, layers - layers // 2]
            arrays = [[held], got]
            if slot:
                arrays = lax.optimization_barrier((arrays, pieces[slot - 1][-1]))[0]
            held, *sent = next_send(arrays, totals if slot == 0 else None, tokens, cuts)
            got = [exchange(send, "mp", bit) for send in sent]
            if slot == 0:
                totals = totals + carried_totals(got[0], tokens)
        pieces.append([[held], got])

    grams, stacked, arrived = [], [], []
    for slot in range(own):
        later = slot + 1 < own
        if later:
            totals = lax.optimization_barrier((totals, pieces[slot + 1][0]))[0]
        rows, gram = stacked_and_gram(pieces[slot], totals, width * mp)
        stacked.append(rows)
        if later:
            gram = lax.optimization_barrier((gram, pieces[slot + 1][1][0]))[0]
        gram, arrived = sum_over_seq(gram, arrived)
        grams.append(gram)
    start = jnp.swapaxes(lax.dynamic_slice_in_dim(start_block, me[0] * own, own, 0), 1, 2)
    return latents_of(start, grams, stacked)


def solution(mesh):
    return jax.shard_map(
        on_device,
        mesh=mesh,
        in_specs=(P(None, "seq", "mp"), P(None, "mp"), P(None, "mp", None), P()),
        out_specs=P("seq", "mp", None),
        check_vma=False,
    )
```

```python
import functools

import jax
import jax.numpy as jnp
from jax import lax
from jax.experimental import pallas as pl
from jax.experimental.pallas import tpu as pltpu
from jax.sharding import PartitionSpec as P

HD = 128
ITERS = 2
EPSILON = 1e-05
F32 = jnp.float32
BF16 = jnp.bfloat16
HIGHEST = lax.Precision.HIGHEST
MIB = 1 << 20


def halving_order(count):
    bits = count.bit_length() - 1
    return sorted(range(count), key=lambda r: int(format(r, f"0{bits}b")[::-1], 2)) if bits else [0]


def exchange(x, axis, bit):
    size = lax.axis_size(axis)
    return lax.ppermute(x, axis, [(j, j ^ bit) for j in range(size)])


def partial_kernel(own, slot, cuts, with_squares, m_ref, gain_ref, hid_ref, w_ref, *refs):
    rows_ref, cols_ref, sems = refs[-3:]
    layers, tokens, width = rows_ref.shape
    mp = cols_ref.shape[2] // HD
    order = halving_order(mp)
    send = [(ref, i) for ref, count in zip(refs[1:], cuts) for i in range(count)]
    copies = {}
    for layer in range(layers):
        here = [pltpu.make_async_copy(hid_ref.at[layer], rows_ref.at[layer], sems.at[layer, 0])]
        for i, r in enumerate(order):
            column = pl.multiple_of((own * (m_ref[0] ^ r) + slot) * HD, HD)
            here.append(
                pltpu.make_async_copy(
                    w_ref.at[layer, :, pl.ds(column, HD)],
                    cols_ref.at[layer, :, pl.ds(i * HD, HD)],
                    sems.at[layer, 1 + i],
                )
            )
        for copy in here:
            copy.start()
        copies[layer] = here
    half = mp // 2 * HD
    gains = gain_ref[...]
    for layer in range(layers):
        copies[layer][0].wait()
        rows = rows_ref[layer]
        scaled = rows * gains[layer : layer + 1]
        for copy in copies[layer][1:]:
            copy.wait()
        total = jnp.dot(scaled, cols_ref[layer], preferred_element_type=F32)
        refs[0][layer] = total[:, :half].astype(BF16)
        ref, i = send[layer]
        ref[i] = total[:, half:].astype(BF16)
        if not with_squares:
            continue
        wide = rows.astype(F32)
        squares = None
        for i in range(width // HD):
            x = wide[:, i * HD : (i + 1) * HD]
            squares = x * x if squares is None else squares + x * x
        refs[1 + len(cuts)][layer : layer + 1, :] = lax.dot_general(
            jnp.ones((8, HD), F32),
            squares,
            (((1,), (1,)), ((), ())),
            precision=HIGHEST,
            preferred_element_type=F32,
        )[:1]


def partial_products(hidden, gains, weights, me, own, slot, cuts, with_squares):
    layers, tokens, width = hidden.shape
    mp = lax.axis_size("mp")
    half = mp // 2 * HD
    outs = [jax.ShapeDtypeStruct((n, tokens, half), BF16) for n in [layers] + cuts]
    outs += [jax.ShapeDtypeStruct((layers, tokens), F32)] * with_squares
    vmem = pl.BlockSpec(memory_space=pltpu.VMEM)
    hbm = pl.BlockSpec(memory_space=pltpu.HBM)
    return pl.pallas_call(
        functools.partial(partial_kernel, own, slot, cuts, with_squares),
        out_shape=outs,
        in_specs=[pl.BlockSpec(memory_space=pltpu.SMEM), vmem, hbm, hbm],
        out_specs=[vmem] * len(outs),
        scratch_shapes=[
            pltpu.VMEM((layers, tokens, width), BF16),
            pltpu.VMEM((layers, width, mp * HD), BF16),
            pltpu.SemaphoreType.DMA((layers, mp + 1)),
        ],
        compiler_params=pltpu.CompilerParams(vmem_limit_bytes=32 * MIB),
        cost_estimate=pl.CostEstimate(
            flops=2 * layers * tokens * width * mp * HD,
            bytes_accessed=layers * width * (tokens + mp * HD) * 2,
            transcendentals=0,
        ),
        name="partial_products",
    )(me, gains, *[pltpu.with_memory_space_constraint(x, pltpu.HBM) for x in (hidden, weights)])


def by_layer(groups, refs):
    parts, at = [], 0
    for counts in groups:
        parts.append([refs[at + n].at[i] for n, count in enumerate(counts) for i in range(count)])
        at += len(counts)
    return parts


def merge_kernel(groups, cuts, tokens, *refs):
    own_ref, out_refs = refs[-1 - len(cuts)], refs[-len(cuts) :]
    layers, _, half = own_ref.shape
    out = [ref.at[i] for ref, count in zip(out_refs, cuts) for i in range(count)]
    parts = by_layer(groups, refs)
    for layer in range(layers):
        total = sum(p[layer][...].astype(F32) for p in parts)
        own_ref[layer] = total[:, :half].astype(BF16)
        out[layer][:tokens, :] = total[:, half:].astype(BF16)
    extra = out_refs[0].shape[1] - tokens
    if extra:
        totals = refs[sum(len(counts) for counts in groups)][...]
        lines = [
            p.astype(F32)
            for layer in range(layers)
            for p in split3(
                jnp.concatenate(
                    [totals[layer : layer + 1, i * HD : (i + 1) * HD] for i in range(tokens // HD)], axis=0
                )
            )
        ]
        out_refs[0][:, tokens:, :] = jnp.zeros((cuts[0], extra, half), BF16)
        out_refs[0][0, tokens:, :HD] = jnp.concatenate(lines, axis=0).astype(BF16)


def next_send(pieces, tokens, cuts, totals):
    groups = [[a.shape[0] for a in group] for group in pieces]
    arrays = [a for group in pieces for a in group]
    layers, width = sum(groups[0]), arrays[0].shape[2]
    half = width // 2
    block = lambda *shape: pl.BlockSpec(shape, lambda i: (0,) * len(shape))
    outs = [(layers, tokens, half)] + [(n, tokens, half) for n in cuts]
    extra = [] if totals is None else [totals]
    if extra:
        outs[1] = (cuts[0], tokens + 3 * layers * (tokens // HD), half)
    return pl.pallas_call(
        functools.partial(merge_kernel, groups, cuts, tokens),
        out_shape=[jax.ShapeDtypeStruct(shape, BF16) for shape in outs],
        grid=(1,),
        in_specs=[block(a.shape[0], tokens, width) for a in arrays] + [block(*t.shape) for t in extra],
        out_specs=[block(*shape) for shape in outs],
        compiler_params=pltpu.CompilerParams(vmem_limit_bytes=16 * MIB),
        name="next_send",
    )(*arrays, *extra)


def carried_totals(received, tokens, layers):
    return received[0, tokens:, :HD].astype(F32).reshape(layers, 3, tokens).sum(1)


def gram_kernel(parts, width, squares_ref, *refs):
    layers = squares_ref.shape[0]
    factor = lax.rsqrt(squares_ref[...] / width + EPSILON)
    factor = jnp.transpose(jnp.concatenate([factor] * (8 // layers), axis=0))
    inputs, outs, gram_ref = refs[: -1 - len(parts)], refs[-1 - len(parts) : -1], refs[-1]
    column, before = 0, None
    for (first, count), stacked_ref in zip(parts, outs):
        held_ref, got_ref, inputs = inputs[0], inputs[1], inputs[2:]
        blocks = []
        for i in range(count):
            total = held_ref[i].astype(F32) + got_ref[i].astype(F32)
            blocks.append((total * factor[:, first + i : first + i + 1]).astype(BF16))
        stacked = jnp.concatenate(blocks, axis=1)
        stacked_ref[...] = stacked
        if first:
            stacked = jnp.concatenate([before, stacked], axis=1)
        before = stacked
        for i, block in enumerate(blocks):
            upto = (first + i + 1) * HD
            gram_ref[:, column : column + upto] = lax.dot_general(
                block, stacked[:, :upto], (((0,), (0,)), ((), ())), preferred_element_type=F32
            ).astype(BF16)
            column += upto


def stacked_and_gram(parts, squares, width):
    layers, tokens = squares.shape
    at = lambda *index: lambda i: index
    arrays, in_specs, out_shape, out_specs, spans = [squares], [pl.BlockSpec(squares.shape, at(0, 0))], [], [], []
    columns = 0
    for held, got, first in parts:
        count = got.shape[0]
        arrays += [held, got]
        in_specs.append(pl.BlockSpec((count, tokens, HD), at(first // count, 0, 0)))
        in_specs.append(pl.BlockSpec((count, tokens, HD), at(0, 0, 0)))
        out_shape.append(pltpu.HBM((tokens, count * HD), BF16))
        out_specs.append(pl.BlockSpec((tokens, count * HD), at(0, 0)))
        spans.append((first, count))
        columns += sum(first + i + 1 for i in range(count)) * HD
    return pl.pallas_call(
        functools.partial(gram_kernel, spans, width),
        out_shape=out_shape + [jax.ShapeDtypeStruct((HD, columns), BF16)],
        grid=(1,),
        in_specs=in_specs,
        out_specs=out_specs + [pl.BlockSpec((HD, columns), at(0, 0))],
        compiler_params=pltpu.CompilerParams(vmem_limit_bytes=16 * MIB),
        name="stacked_gram",
    )(*arrays)


def sum_over_seq(x):
    size = lax.axis_size("seq")
    me = lax.axis_index("seq")
    bits = [1 << i for i in range(size.bit_length() - 1)]
    for bit in bits[:-1]:
        half = x.shape[0] // 2
        mine = jnp.where((me & bit) != 0, half, 0)
        got = exchange(lax.dynamic_slice_in_dim(x, half - mine, half, 0).astype(BF16), "seq", bit)
        x = lax.dynamic_slice_in_dim(x, mine, half, 0).astype(F32) + got.astype(F32)
    x = x.astype(BF16)
    x = (x.astype(F32) + exchange(x, "seq", bits[-1]).astype(F32)).astype(BF16)
    for bit in bits[:-1][::-1]:
        got = exchange(x, "seq", bit)
        upper = (me & bit) != 0
        x = jnp.concatenate([jnp.where(upper, got, x), jnp.where(upper, x, got)], axis=0)
    return x


def split3(x):
    high = x.astype(BF16)
    rest = x - high.astype(F32)
    middle = rest.astype(BF16)
    return high, middle, (rest - middle.astype(F32)).astype(BF16)


def rank_update(x):
    h, m, l = split3(x)
    left = jnp.concatenate([h, h, m, h, m, l], axis=0)
    right = jnp.concatenate([h, m, h, l, m, h], axis=0)
    return lax.dot_general(left, right, (((0,), (0,)), ((), ())), preferred_element_type=F32)


def reciprocal(d):
    r = pl.reciprocal(d, approx=True)
    return r * (2.0 - d * r)


def factor_panel(rows, base):
    b, n = rows.shape
    lane = lax.broadcasted_iota(jnp.int32, (8, n), 1)
    row = lax.broadcasted_iota(jnp.int32, (8, n), 0)

    def spread(x, k):
        return jnp.broadcast_to(x[k : k + 1, :], (8, n))

    tiles = [rows[i : i + 8] for i in range(0, b, 8)]
    columns = [[jnp.broadcast_to(t[:, base + j : base + j + 1], (8, n)) for t in tiles] for j in range(b)]
    pivots = [jnp.zeros((8, n), F32) for _ in tiles]
    for k in range(b):
        top, at = k // 8, k % 8
        pivot = spread(columns[k][top], at)
        pivots[top] = jnp.where(row == at, pivot, pivots[top])
        here = lane == base + k
        tiles[top] = jnp.where(here & (row >= at), jnp.where(row == at, 1.0, 0.0), tiles[top])
        if k == b - 1:
            break
        inverse = reciprocal(pivot)
        chosen = spread(tiles[top], at)
        others = [spread(columns[j][top], at) for j in range(k + 1, b)]
        for i in range(top, len(tiles)):
            multiplier = columns[k][i] * inverse
            if i == top:
                multiplier = jnp.where(row > at, multiplier, 0.0)
            else:
                tiles[i] = jnp.where(here, 0.0, tiles[i])
            tiles[i] = tiles[i] - multiplier * chosen
            for j in range(k + 1, b):
                columns[j][i] = columns[j][i] - multiplier * others[j - k - 1]
    for i in range(len(tiles)):
        tiles[i] = jnp.where((lane > base + 8 * i + row) & (lane < base + b), 0.0, tiles[i])
        tiles[i] = tiles[i] * lax.rsqrt(pivots[i])
    return jnp.concatenate(tiles, axis=0)


def inverse_cholesky(matrices, b=16):
    n = matrices[0].shape[0]
    panels = [[] for _ in matrices]
    rests = list(matrices)
    lane = lax.broadcasted_iota(jnp.int32, (n, n), 1)
    row = lax.broadcasted_iota(jnp.int32, (n, n), 0)
    for base in range(0, n, b):
        for s, rest in enumerate(rests):
            panels[s].append(factor_panel(rest[:b], base))
        if base + b < n:
            for s, rest in enumerate(rests):
                update = rank_update(panels[s][-1])[base + b :]
                rest = rest[b:]
                at = lane[: rest.shape[0]]
                rests[s] = jnp.where((at >= base) & (at < base + b), 0.0, rest) - update
    return [jnp.where(lane <= row, jnp.concatenate(p, axis=0), 0.0) for p in panels]


def basis_kernel(own, layers, chains, start_ref, *refs):
    grams_in = refs[: len(chains)]
    stacked_in = refs[len(chains) : -3]
    out_ref, rows_ref, sems = refs[-3:]
    block, copies = {}, [[] for _ in range(own)]
    at = 0
    for chain, ref in zip(chains, grams_in):
        column = 0
        for slot, first, count in chain:
            to = rows_ref.at[slot, :, pl.ds(first * HD, count * HD)]
            copies[slot].append(pltpu.make_async_copy(stacked_in[at], to, sems.at[at]))
            at += 1
            for i in range(first, first + count):
                for j in range(i + 1):
                    block[slot, i, j] = ref[:, column : column + HD]
                    column += HD
    for copy in sum(copies, []):
        copy.start()
    grams = []
    for slot in range(own):
        rows = [
            jnp.concatenate(
                [
                    block[slot, i, j] if j <= i else jnp.transpose(block[slot, j, i].astype(F32)).astype(BF16)
                    for j in range(layers)
                ],
                axis=1,
            )
            for i in range(layers)
        ]
        grams.append(jnp.concatenate(rows, axis=0))
    rank = start_ref.shape[1]

    def through_gram(x, gram):
        y = jnp.dot(jnp.concatenate(split3(x), axis=0), gram, preferred_element_type=F32)
        return y[:rank] + y[rank : 2 * rank] + y[2 * rank :]

    images = [jnp.dot(start_ref[s], grams[s], preferred_element_type=F32) for s in range(own)]
    for step in range(ITERS):
        inner = [
            lax.dot_general(x, x, (((1,), (1,)), ((), ())), precision=HIGHEST, preferred_element_type=F32)
            for x in images
        ]
        if step < ITERS - 1:
            images = [through_gram(x, g) for x, g in zip(images, grams)]
        images = [
            jnp.dot(f, x, precision=HIGHEST, preferred_element_type=F32)
            for x, f in zip(images, inverse_cholesky(inner))
        ]
    for s in range(own):
        for copy in copies[s]:
            copy.wait()
        out_ref[:, s, :] = lax.dot_general(
            rows_ref[s], images[s].astype(BF16), (((1,), (1,)), ((), ())), preferred_element_type=F32
        ).astype(BF16)


def latents_of(start, chains, grams, stacked, tokens, layers):
    own = start.shape[0]
    whole = lambda a: pl.BlockSpec(a.shape, lambda i: (0,) * a.ndim)
    return pl.pallas_call(
        functools.partial(basis_kernel, own, layers, chains),
        out_shape=jax.ShapeDtypeStruct((tokens, own, HD), BF16),
        grid=(1,),
        in_specs=[whole(a) for a in [start] + grams] + [pl.BlockSpec(memory_space=pltpu.HBM)] * len(stacked),
        out_specs=pl.BlockSpec((tokens, own, HD), lambda i: (0, 0, 0)),
        scratch_shapes=[
            pltpu.VMEM((own, tokens, layers * HD), BF16),
            pltpu.SemaphoreType.DMA((len(stacked),)),
        ],
        compiler_params=pltpu.CompilerParams(vmem_limit_bytes=16 * MIB),
        name="basis_latents",
    )(start, *grams, *[pltpu.with_memory_space_constraint(x, pltpu.HBM) for x in stacked])


def on_device(hidden, norm_gain, proj_weight, start_block):
    layers, tokens, width = hidden.shape
    mp = lax.axis_size("mp")
    own = proj_weight.shape[2] // HD // mp
    me = lax.axis_index("mp").astype(jnp.int32).reshape(1)
    mp_bits = [1 << i for i in range(mp.bit_length() - 1)]

    half = layers // 2
    held, got, sent = [None] * own, [None] * own, []
    for slot in range(own):
        last = slot == own - 1
        here = me if slot == 0 else lax.optimization_barrier((me, sent[-1]))[0]
        cuts = [half, layers - half] if last else [layers]
        parcels = [1] * layers if last else cuts
        held[slot], *sent = partial_products(hidden, norm_gain, proj_weight, here, own, slot, parcels, last)
        if last:
            totals = sent.pop()
            totals = totals + exchange(totals, "mp", 1)
        got[slot] = [exchange(send, "mp", 1) for send in sent]
        for bit in mp_bits[1:]:
            pieces = [[held[slot]], got[slot]]
            if slot:
                pieces = lax.optimization_barrier((pieces, got[slot - 1]))[0]
            held[slot], *sent = next_send(pieces, tokens, cuts, totals if last else None)
            got[slot] = [exchange(send, "mp", bit) for send in sent]
            if last:
                totals = totals + carried_totals(got[slot][0], tokens, layers)

    chains = [[(slot, 0, layers)] for slot in range(own - 1)]
    chains.append([(own - 1, 0, half), (own - 1, half, layers - half)])
    grams, stacked = [], []
    for chain in chains:
        parts = [
            (held[slot], got[slot][1 if first else 0], first)
            for slot, first, _ in chain
        ]
        *rows, gram = stacked_and_gram(parts, totals, width * mp)
        stacked += rows
        grams.append(sum_over_seq(gram))
    start = jnp.swapaxes(lax.dynamic_slice_in_dim(start_block, me[0] * own, own, 0), 1, 2)
    return latents_of(start, chains, grams, stacked, tokens, layers)


def solution(mesh):
    return jax.shard_map(
        on_device,
        mesh=mesh,
        in_specs=(P(None, "seq", "mp"), P(None, "mp"), P(None, "mp", None), P()),
        out_specs=P("seq", "mp", None),
        check_vma=False,
    )
```

```python
import functools

import jax
import jax.numpy as jnp
from jax import lax
from jax.experimental import pallas as pl
from jax.experimental.pallas import tpu as pltpu
from jax.sharding import PartitionSpec as P

HD = 128
ITERS = 2
EPSILON = 1e-05
F32 = jnp.float32
BF16 = jnp.bfloat16
HIGHEST = lax.Precision.HIGHEST
MIB = 1 << 20


def halving_order(count):
    bits = count.bit_length() - 1
    return sorted(range(count), key=lambda r: int(format(r, f"0{bits}b")[::-1], 2)) if bits else [0]


def exchange(x, axis, bit):
    size = lax.axis_size(axis)
    return lax.ppermute(x, axis, [(j, j ^ bit) for j in range(size)])


def partial_kernel(own, slot, cuts, with_squares, m_ref, gain_ref, hid_ref, w_ref, *refs):
    rows_ref, cols_ref, sems = refs[-3:]
    layers, tokens, width = rows_ref.shape
    mp = cols_ref.shape[2] // HD
    order = halving_order(mp)
    send = [(ref, i) for ref, count in zip(refs[1:], cuts) for i in range(count)]
    copies = {}
    for layer in range(layers):
        here = [pltpu.make_async_copy(hid_ref.at[layer], rows_ref.at[layer], sems.at[layer, 0])]
        for i, r in enumerate(order):
            column = pl.multiple_of((own * (m_ref[0] ^ r) + slot) * HD, HD)
            here.append(
                pltpu.make_async_copy(
                    w_ref.at[layer, :, pl.ds(column, HD)],
                    cols_ref.at[layer, :, pl.ds(i * HD, HD)],
                    sems.at[layer, 1 + i],
                )
            )
        for copy in here:
            copy.start()
        copies[layer] = here
    half = mp // 2 * HD
    gains = gain_ref[...]
    for layer in range(layers):
        copies[layer][0].wait()
        rows = rows_ref[layer]
        scaled = rows * gains[layer : layer + 1]
        if with_squares:
            wide = rows.astype(F32)
            squares = None
            for i in range(width // HD):
                x = wide[:, i * HD : (i + 1) * HD]
                squares = x * x if squares is None else squares + x * x
            refs[1 + len(cuts)][layer : layer + 1, :] = lax.dot_general(
                jnp.ones((8, HD), F32),
                squares,
                (((1,), (1,)), ((), ())),
                precision=HIGHEST,
                preferred_element_type=F32,
            )[:1]
        for copy in copies[layer][1:]:
            copy.wait()
        total = jnp.dot(scaled, cols_ref[layer], preferred_element_type=F32)
        refs[0][layer] = total[:, :half].astype(BF16)
        ref, i = send[layer]
        ref[i] = total[:, half:].astype(BF16)


def partial_products(hidden, gains, weights, me, own, slot, cuts, with_squares):
    layers, tokens, width = hidden.shape
    mp = lax.axis_size("mp")
    half = mp // 2 * HD
    outs = [jax.ShapeDtypeStruct((n, tokens, half), BF16) for n in [layers] + cuts]
    outs += [jax.ShapeDtypeStruct((layers, tokens), F32)] * with_squares
    vmem = pl.BlockSpec(memory_space=pltpu.VMEM)
    hbm = pl.BlockSpec(memory_space=pltpu.HBM)
    return pl.pallas_call(
        functools.partial(partial_kernel, own, slot, cuts, with_squares),
        out_shape=outs,
        in_specs=[pl.BlockSpec(memory_space=pltpu.SMEM), vmem, hbm, hbm],
        out_specs=[vmem] * len(outs),
        scratch_shapes=[
            pltpu.VMEM((layers, tokens, width), BF16),
            pltpu.VMEM((layers, width, mp * HD), BF16),
            pltpu.SemaphoreType.DMA((layers, mp + 1)),
        ],
        compiler_params=pltpu.CompilerParams(vmem_limit_bytes=32 * MIB),
        cost_estimate=pl.CostEstimate(
            flops=2 * layers * tokens * width * mp * HD,
            bytes_accessed=layers * width * (tokens + mp * HD) * 2,
            transcendentals=0,
        ),
        name="partial_products",
    )(me, gains, *[pltpu.with_memory_space_constraint(x, pltpu.HBM) for x in (hidden, weights)])


def by_layer(groups, refs):
    parts, at = [], 0
    for counts in groups:
        parts.append([refs[at + n].at[i] for n, count in enumerate(counts) for i in range(count)])
        at += len(counts)
    return parts


def merge_kernel(groups, cuts, tokens, *refs):
    own_ref, out_refs = refs[-1 - len(cuts)], refs[-len(cuts) :]
    layers, _, half = own_ref.shape
    out = [ref.at[i] for ref, count in zip(out_refs, cuts) for i in range(count)]
    parts = by_layer(groups, refs)
    for layer in range(layers):
        total = sum(p[layer][...].astype(F32) for p in parts)
        own_ref[layer] = total[:, :half].astype(BF16)
        out[layer][:tokens, :] = total[:, half:].astype(BF16)
    extra = out_refs[0].shape[1] - tokens
    if extra:
        totals = refs[sum(len(counts) for counts in groups)][...]
        lines = [
            p.astype(F32)
            for layer in range(layers)
            for p in split3(
                jnp.concatenate(
                    [totals[layer : layer + 1, i * HD : (i + 1) * HD] for i in range(tokens // HD)], axis=0
                )
            )
        ]
        out_refs[0][:, tokens:, :] = jnp.zeros((cuts[0], extra, half), BF16)
        out_refs[0][0, tokens:, :HD] = jnp.concatenate(lines, axis=0).astype(BF16)


def next_send(pieces, tokens, cuts, totals):
    groups = [[a.shape[0] for a in group] for group in pieces]
    arrays = [a for group in pieces for a in group]
    layers, width = sum(groups[0]), arrays[0].shape[2]
    half = width // 2
    block = lambda *shape: pl.BlockSpec(shape, lambda i: (0,) * len(shape))
    outs = [(layers, tokens, half)] + [(n, tokens, half) for n in cuts]
    extra = [] if totals is None else [totals]
    if extra:
        outs[1] = (cuts[0], tokens + 3 * layers * (tokens // HD), half)
    return pl.pallas_call(
        functools.partial(merge_kernel, groups, cuts, tokens),
        out_shape=[jax.ShapeDtypeStruct(shape, BF16) for shape in outs],
        grid=(1,),
        in_specs=[block(a.shape[0], tokens, width) for a in arrays] + [block(*t.shape) for t in extra],
        out_specs=[block(*shape) for shape in outs],
        compiler_params=pltpu.CompilerParams(vmem_limit_bytes=16 * MIB),
        name="next_send",
    )(*arrays, *extra)


def carried_totals(received, tokens, layers):
    return received[0, tokens:, :HD].astype(F32).reshape(layers, 3, tokens).sum(1)


def gram_kernel(parts, width, squares_ref, *refs):
    layers = squares_ref.shape[0]
    factor = lax.rsqrt(squares_ref[...] / width + EPSILON)
    factor = jnp.transpose(jnp.concatenate([factor] * (8 // layers), axis=0))
    inputs, outs, gram_ref = refs[: -1 - len(parts)], refs[-1 - len(parts) : -1], refs[-1]
    column, before = 0, None
    for (first, count), stacked_ref in zip(parts, outs):
        held_ref, got_ref, inputs = inputs[0], inputs[1], inputs[2:]
        blocks = []
        for i in range(count):
            total = held_ref[i].astype(F32) + got_ref[i].astype(F32)
            blocks.append((total * factor[:, first + i : first + i + 1]).astype(BF16))
        stacked = jnp.concatenate(blocks, axis=1)
        stacked_ref[...] = stacked
        if first:
            stacked = jnp.concatenate([before, stacked], axis=1)
        before = stacked
        for i, block in enumerate(blocks):
            upto = (first + i + 1) * HD
            gram_ref[:, column : column + upto] = lax.dot_general(
                block, stacked[:, :upto], (((0,), (0,)), ((), ())), preferred_element_type=F32
            ).astype(BF16)
            column += upto


def stacked_and_gram(parts, squares, width):
    layers, tokens = squares.shape
    at = lambda *index: lambda i: index
    arrays, in_specs, out_shape, out_specs, spans = [squares], [pl.BlockSpec(squares.shape, at(0, 0))], [], [], []
    columns = 0
    for held, got, first in parts:
        count = got.shape[0]
        arrays += [held, got]
        in_specs.append(pl.BlockSpec((count, tokens, HD), at(first // count, 0, 0)))
        in_specs.append(pl.BlockSpec((count, tokens, HD), at(0, 0, 0)))
        out_shape.append(pltpu.HBM((tokens, count * HD), BF16))
        out_specs.append(pl.BlockSpec((tokens, count * HD), at(0, 0)))
        spans.append((first, count))
        columns += sum(first + i + 1 for i in range(count)) * HD
    return pl.pallas_call(
        functools.partial(gram_kernel, spans, width),
        out_shape=out_shape + [jax.ShapeDtypeStruct((HD, columns), BF16)],
        grid=(1,),
        in_specs=in_specs,
        out_specs=out_specs + [pl.BlockSpec((HD, columns), at(0, 0))],
        compiler_params=pltpu.CompilerParams(vmem_limit_bytes=16 * MIB),
        name="stacked_gram",
    )(*arrays)


def sum_over_seq(x):
    size = lax.axis_size("seq")
    me = lax.axis_index("seq")
    bits = [1 << i for i in range(size.bit_length() - 1)]
    for bit in bits[:-1]:
        half = x.shape[0] // 2
        mine = jnp.where((me & bit) != 0, half, 0)
        got = exchange(lax.dynamic_slice_in_dim(x, half - mine, half, 0).astype(BF16), "seq", bit)
        x = lax.dynamic_slice_in_dim(x, mine, half, 0).astype(F32) + got.astype(F32)
    x = x.astype(BF16)
    x = (x.astype(F32) + exchange(x, "seq", bits[-1]).astype(F32)).astype(BF16)
    for bit in bits[:-1][::-1]:
        got = exchange(x, "seq", bit)
        upper = (me & bit) != 0
        x = jnp.concatenate([jnp.where(upper, got, x), jnp.where(upper, x, got)], axis=0)
    return x


def split3(x):
    high = x.astype(BF16)
    rest = x - high.astype(F32)
    middle = rest.astype(BF16)
    return high, middle, (rest - middle.astype(F32)).astype(BF16)


def rank_update(x):
    h, m, l = split3(x)
    left = jnp.concatenate([h, h, m, h, m, l], axis=0)
    right = jnp.concatenate([h, m, h, l, m, h], axis=0)
    return lax.dot_general(left, right, (((0,), (0,)), ((), ())), preferred_element_type=F32)


def reciprocal(d):
    r = pl.reciprocal(d, approx=True)
    return r * (2.0 - d * r)


def factor_panel(rows, base):
    b, n = rows.shape
    lane = lax.broadcasted_iota(jnp.int32, (8, n), 1)
    row = lax.broadcasted_iota(jnp.int32, (8, n), 0)

    def spread(x, k):
        return jnp.broadcast_to(x[k : k + 1, :], (8, n))

    tiles = [rows[i : i + 8] for i in range(0, b, 8)]
    columns = [[jnp.broadcast_to(t[:, base + j : base + j + 1], (8, n)) for t in tiles] for j in range(b)]
    pivots = [jnp.zeros((8, n), F32) for _ in tiles]
    for k in range(b):
        top, at = k // 8, k % 8
        pivot = spread(columns[k][top], at)
        pivots[top] = jnp.where(row == at, pivot, pivots[top])
        here = lane == base + k
        tiles[top] = jnp.where(here & (row >= at), jnp.where(row == at, 1.0, 0.0), tiles[top])
        if k == b - 1:
            break
        inverse = reciprocal(pivot)
        chosen = spread(tiles[top], at)
        others = [spread(columns[j][top], at) for j in range(k + 1, b)]
        for i in range(top, len(tiles)):
            multiplier = columns[k][i] * inverse
            if i == top:
                multiplier = jnp.where(row > at, multiplier, 0.0)
            else:
                tiles[i] = jnp.where(here, 0.0, tiles[i])
            tiles[i] = tiles[i] - multiplier * chosen
            for j in range(k + 1, b):
                columns[j][i] = columns[j][i] - multiplier * others[j - k - 1]
    for i in range(len(tiles)):
        tiles[i] = jnp.where((lane > base + 8 * i + row) & (lane < base + b), 0.0, tiles[i])
        tiles[i] = tiles[i] * lax.rsqrt(pivots[i])
    return jnp.concatenate(tiles, axis=0)


def inverse_cholesky(matrices, b=16):
    n = matrices[0].shape[0]
    panels = [[] for _ in matrices]
    rests = list(matrices)
    lane = lax.broadcasted_iota(jnp.int32, (n, n), 1)
    row = lax.broadcasted_iota(jnp.int32, (n, n), 0)
    for base in range(0, n, b):
        for s, rest in enumerate(rests):
            panels[s].append(factor_panel(rest[:b], base))
        if base + b < n:
            for s, rest in enumerate(rests):
                update = rank_update(panels[s][-1])[base + b :]
                rest = rest[b:]
                at = lane[: rest.shape[0]]
                rests[s] = jnp.where((at >= base) & (at < base + b), 0.0, rest) - update
    return [jnp.where(lane <= row, jnp.concatenate(p, axis=0), 0.0) for p in panels]


def basis_kernel(own, layers, chains, start_ref, *refs):
    grams_in = refs[: len(chains)]
    stacked_in = refs[len(chains) : -3]
    out_ref, rows_ref, sems = refs[-3:]
    block, copies = {}, [[] for _ in range(own)]
    at = 0
    for chain, ref in zip(chains, grams_in):
        column = 0
        for slot, first, count in chain:
            to = rows_ref.at[slot, :, pl.ds(first * HD, count * HD)]
            copies[slot].append(pltpu.make_async_copy(stacked_in[at], to, sems.at[at]))
            at += 1
            for i in range(first, first + count):
                for j in range(i + 1):
                    block[slot, i, j] = ref[:, column : column + HD]
                    column += HD
    for copy in sum(copies, []):
        copy.start()
    grams = []
    for slot in range(own):
        rows = [
            jnp.concatenate(
                [
                    block[slot, i, j] if j <= i else jnp.transpose(block[slot, j, i].astype(F32)).astype(BF16)
                    for j in range(layers)
                ],
                axis=1,
            )
            for i in range(layers)
        ]
        grams.append(jnp.concatenate(rows, axis=0))
    rank = start_ref.shape[1]

    def through_gram(x, gram):
        y = jnp.dot(jnp.concatenate(split3(x), axis=0), gram, preferred_element_type=F32)
        return y[:rank] + y[rank : 2 * rank] + y[2 * rank :]

    images = [jnp.dot(start_ref[s], grams[s], preferred_element_type=F32) for s in range(own)]
    for step in range(ITERS):
        inner = [
            lax.dot_general(x, x, (((1,), (1,)), ((), ())), precision=HIGHEST, preferred_element_type=F32)
            for x in images
        ]
        if step < ITERS - 1:
            images = [through_gram(x, g) for x, g in zip(images, grams)]
        images = [
            jnp.dot(f, x, precision=HIGHEST, preferred_element_type=F32)
            for x, f in zip(images, inverse_cholesky(inner))
        ]
    for s in range(own):
        for copy in copies[s]:
            copy.wait()
        out_ref[:, s, :] = lax.dot_general(
            rows_ref[s], images[s].astype(BF16), (((1,), (1,)), ((), ())), preferred_element_type=F32
        ).astype(BF16)


def latents_of(start, chains, grams, stacked, tokens, layers):
    own = start.shape[0]
    whole = lambda a: pl.BlockSpec(a.shape, lambda i: (0,) * a.ndim)
    return pl.pallas_call(
        functools.partial(basis_kernel, own, layers, chains),
        out_shape=jax.ShapeDtypeStruct((tokens, own, HD), BF16),
        grid=(1,),
        in_specs=[whole(a) for a in [start] + grams] + [pl.BlockSpec(memory_space=pltpu.HBM)] * len(stacked),
        out_specs=pl.BlockSpec((tokens, own, HD), lambda i: (0, 0, 0)),
        scratch_shapes=[
            pltpu.VMEM((own, tokens, layers * HD), BF16),
            pltpu.SemaphoreType.DMA((len(stacked),)),
        ],
        compiler_params=pltpu.CompilerParams(vmem_limit_bytes=16 * MIB),
        name="basis_latents",
    )(start, *grams, *[pltpu.with_memory_space_constraint(x, pltpu.HBM) for x in stacked])


def on_device(hidden, norm_gain, proj_weight, start_block):
    layers, tokens, width = hidden.shape
    mp = lax.axis_size("mp")
    own = proj_weight.shape[2] // HD // mp
    me = lax.axis_index("mp").astype(jnp.int32).reshape(1)
    mp_bits = [1 << i for i in range(mp.bit_length() - 1)]

    half = layers // 2
    held, got, sent = [None] * own, [None] * own, []
    for slot in range(own):
        last = slot == own - 1
        here = me if slot == 0 else lax.optimization_barrier((me, sent[-1]))[0]
        cuts = [half, layers - half] if last else [layers]
        parcels = [1] * layers if last else cuts
        held[slot], *sent = partial_products(hidden, norm_gain, proj_weight, here, own, slot, parcels, last)
        if last:
            totals = sent.pop()
            totals = totals + exchange(totals, "mp", 1)
        got[slot] = [exchange(send, "mp", 1) for send in sent]
        for bit in mp_bits[1:]:
            pieces = [[held[slot]], got[slot]]
            if slot:
                pieces = lax.optimization_barrier((pieces, got[slot - 1]))[0]
            held[slot], *sent = next_send(pieces, tokens, cuts, totals if last else None)
            got[slot] = [exchange(send, "mp", bit) for send in sent]
            if last:
                totals = totals + carried_totals(got[slot][0], tokens, layers)

    chains = [[(slot, 0, layers)] for slot in range(own - 1)]
    chains.append([(own - 1, 0, half), (own - 1, half, layers - half)])
    grams, stacked = [], []
    for chain in chains:
        parts = [
            (held[slot], got[slot][1 if first else 0], first)
            for slot, first, _ in chain
        ]
        *rows, gram = stacked_and_gram(parts, totals, width * mp)
        stacked += rows
        grams.append(sum_over_seq(gram))
    start = jnp.swapaxes(lax.dynamic_slice_in_dim(start_block, me[0] * own, own, 0), 1, 2)
    return latents_of(start, chains, grams, stacked, tokens, layers)


def solution(mesh):
    return jax.shard_map(
        on_device,
        mesh=mesh,
        in_specs=(P(None, "seq", "mp"), P(None, "mp"), P(None, "mp", None), P()),
        out_specs=P("seq", "mp", None),
        check_vma=False,
    )
```
